256 devices in a mesh: dp: 16 (over z, x_hi), fsdp: 16 (over y, x_lo, core).
Axes of the slice: x: 4 (x_hi: 2, x_lo: 2; x = x_hi * 2 + x_lo), y: 4, z: 8, core: 2. Of those that a mesh axis runs over, the one named last changes fastest.
Arguments:
- inputs: bfloat16 [1024, 14, 14, 256], P(('dp', 'fsdp')), may hold values from -6 to 6
- out_grads: bfloat16 [1024, 14, 14, 256], P(('dp', 'fsdp')), may hold values from -6 to 6
- patch_basis: bfloat16 [1152, 2304], P(None, 'fsdp'), may hold values from -0.1875 to 0.1875
- output_basis: bfloat16 [256, 256], P(None, 'fsdp'), may hold values from -0.375 to 0.375
Outputs:
- second_moment: float32 [256, 2304], P('dp', 'fsdp')
- scaled_sum: float32 [256, 2304], P('dp', 'fsdp')
The draws below stay inside these ranges and needn't reach their ends.
All inputs are finite; a program needn't handle non-finite values.
Results may differ from the reference program's by a relative error of at most 0.0041.
Values may be sent and summed in bfloat16 or wider, within the bound.
No kernel may reach another device: no remote copies, remote signals or barrier semaphores. Data moves between devices by JAX's collectives and lax.ppermute only.
A program may use at most 64 MiB of HBM per device.

```python
import math
import jax
import jax.numpy as jnp
from jax import lax

C = 256
OUTC = 256
SIDE = 14
P_SIZE = 2304
HALF = 1152
EXAMPLES = 1024


def steps_of(key, shape, split, least, high):
    level = 1.0
    for axis_at, blocks in split:
        steps = jax.random.uniform(jax.random.fold_in(jax.random.fold_in(key, 6), axis_at), (blocks,), jnp.float32, least / len(split), high / len(split))
        level = level * jnp.repeat(jnp.exp(steps), shape[axis_at] // blocks).reshape((-1,) + (1,) * (len(shape) - 1 - axis_at))
    return level


def gaussian(own_key, shape, scale, reach, shards=(), held_as=jnp.bfloat16):
    values = scale * jax.random.normal(own_key, shape, jnp.float32)
    if shards:
        values = values * steps_of(own_key, shape, shards, -0.22, 0.18)
    return jnp.clip(values, -reach, reach).astype(held_as)


def setup_inputs(seed: int = 0) -> dict:
    key_of = jax.random.split(jax.random.key(seed), 5)
    inputs = gaussian(key_of[0], (EXAMPLES, SIDE, SIDE, C), 1.0, 6.0, ((0, 256),))
    out_grads = gaussian(key_of[1], (EXAMPLES, SIDE, SIDE, OUTC), 1.0, 6.0, ((0, 256),))
    patch_basis = gaussian(key_of[2], (HALF, P_SIZE), HALF ** -0.5, 0.1875, ((1, 16),))
    output_basis = gaussian(key_of[3], (OUTC, OUTC), OUTC ** -0.5, 0.375, ((1, 16),))
    return {"inputs": inputs, "out_grads": out_grads, "patch_basis": patch_basis, "output_basis": output_basis}


def patch_rows(feature_maps):
    count = feature_maps.shape[0]
    grid_side = feature_maps.shape[1]
    padded = jnp.pad(feature_maps, ((0, 0), (1, 1), (1, 1), (0, 0)))
    shifted = [padded[:, row_tap:row_tap + grid_side, col_tap:col_tap + grid_side, :] for row_tap in range(3) for col_tap in range(3)]
    return jnp.concatenate(shifted, axis=3).reshape(count, grid_side * grid_side, -1)

def reference(inputs, out_grads, patch_basis, output_basis):
    block_width = patch_basis.shape[0]

    def accumulate(carried, sample):
        example_input, example_grad = sample
        patches = patch_rows(example_input[None])[0]
        low_part = jnp.dot(patches[:, :block_width], patch_basis[:, :block_width], preferred_element_type=jnp.float32)
        high_part = jnp.dot(patches[:, block_width:], patch_basis[:, block_width:], preferred_element_type=jnp.float32)
        rotated = jnp.concatenate([low_part, high_part], axis=1).astype(jnp.bfloat16)
        grad_rot = jnp.dot(example_grad.reshape(-1, OUTC), output_basis, preferred_element_type=jnp.float32).astype(jnp.bfloat16)
        projected = jnp.dot(grad_rot.T, rotated, preferred_element_type=jnp.float32) * (1.0 / SIDE)
        return ((carried[0] + projected * projected, carried[1] + projected), None)
    empty_sums = jnp.zeros((OUTC, 9 * C), jnp.float32)
    (squares, linear), unused = lax.scan(accumulate, (empty_sums, empty_sums), (inputs, out_grads))
    return (squares / EXAMPLES, linear * (1.0 / math.sqrt(EXAMPLES)))
```

```python
import functools
import math

import jax
import jax.numpy as jnp
from jax import lax
from jax.experimental import pallas as pl
from jax.experimental.pallas import tpu as pltpu
from jax.sharding import Mesh, PartitionSpec as P

AXES = ("z", "xh", "y", "xl", "c")
SIZES = (8, 2, 4, 2, 2)
BF16 = jnp.bfloat16
F32 = jnp.float32
CONTRACT_LAST = (((1,), (1,)), ((), ()))


def ring(value, axis, size, step):
    return lax.ppermute(value, axis, [(i, (i + step) % size) for i in range(size)])


def swap_cores(value):
    return lax.ppermute(value, "c", [(0, 1), (1, 0)])


def swap_x(value):
    def partner(x, core):
        return (x + 1 if (x + core) % 2 == 0 else x - 1) % 4

    pairs = [(x * 2 + core, partner(x, core) * 2 + core) for x in range(4) for core in range(2)]
    return lax.ppermute(value, ("xh", "xl", "c"), pairs)


def prepare(inputs, out_grads):
    both = jnp.stack([inputs, out_grads])
    padded = jnp.pad(both, ((0, 0), (0, 0), (0, 0), (0, 2), (0, 0)))
    return padded.reshape(2, inputs.shape[0], 224, 256)


def moments_kernel(
    at_ref, own, other, far, far_other, s0, sp, sm, s2a, s2b, u_ref,
    squares_ref, linear_ref, basis, rows, patches, out_basis,
):
    y = at_ref[0]
    half = s0.shape[0] // 2

    def place(step, value):
        owner = lax.rem(y + step, 4)
        basis[owner // 2, pl.ds(pl.multiple_of((owner % 2) * 144, 16), 144), :] = value

    place(0, s0[...])
    place(1, sp[...])
    place(3, sm[...])
    place(2, jnp.concatenate([s2a[...], s2b[...]], axis=0))
    for piece in range(16):
        at = pl.multiple_of(at_ref[1 + piece], 16)
        out_basis[pl.ds(at, 16), :] = u_ref[16 * piece : 16 * piece + 16, :]
    rows[...] = jnp.zeros_like(rows)
    squares_ref[...] = jnp.zeros_like(squares_ref)
    linear_ref[...] = jnp.zeros_like(linear_ref)

    for group in (own, other, far, far_other):

        @pl.loop(0, 4)
        def _(n, group=group):
            feature = group[0, n].astype(F32)
            rows[0, 16:240, :] = pltpu.roll(feature, 1, 0).astype(BF16)
            rows[1, 16:240, :] = group[0, n]
            rows[2, 16:240, :] = pltpu.roll(feature, 223, 0).astype(BF16)
            for tap in range(9):
                ky, kx = tap // 3, tap % 3
                shifted = rows[kx, 16 * ky : 16 * ky + 224, :]
                if tap < 4:
                    patches[0, :, 256 * tap : 256 * tap + 256] = shifted
                elif tap == 4:
                    patches[0, :, 1024:1152] = shifted[:, :128]
                    patches[1, :, 0:128] = shifted[:, 128:]
                else:
                    patches[1, :, 256 * tap - 1152 : 256 * tap - 896] = shifted
            grad_rot = lax.dot_general(
                group[1, n], out_basis[...], CONTRACT_LAST, preferred_element_type=F32
            ).astype(BF16)
            for block in range(2):
                rotated = lax.dot_general(
                    basis[block], patches[block], CONTRACT_LAST, preferred_element_type=F32
                ).astype(BF16)
                projected = jnp.dot(rotated, grad_rot, preferred_element_type=F32)
                squares_ref[block] += projected * projected
                linear_ref[block] += projected


def moments(at, *operands):
    shape = jax.ShapeDtypeStruct((2, 288, 256), F32)
    vmem = pl.BlockSpec(memory_space=pltpu.VMEM)
    return pl.pallas_call(
        moments_kernel,
        out_shape=(shape, shape),
        in_specs=[pl.BlockSpec(memory_space=pltpu.SMEM)] + [vmem] * len(operands),
        out_specs=(vmem, vmem),
        scratch_shapes=[
            pltpu.VMEM((2, 288, 1152), BF16),
            pltpu.VMEM((3, 256, 256), BF16),
            pltpu.VMEM((2, 224, 1152), BF16),
            pltpu.VMEM((256, 256), BF16),
        ],
        compiler_params=pltpu.CompilerParams(vmem_limit_bytes=40 * 2**20),
        name="moments",
    )(at, *operands)


def on_device(inputs, out_grads, patch_basis, output_basis):
    examples = inputs.shape[0] * math.prod(SIZES)
    y, xl, core = lax.axis_index("y"), lax.axis_index("xl"), lax.axis_index("c")

    own = prepare(inputs, out_grads)
    other = swap_cores(own)
    u0 = output_basis.T
    u1 = jnp.concatenate([u0, swap_cores(u0)])
    far = swap_x(own)
    s0 = patch_basis.T
    sp, sm = ring(s0, "y", 4, 3), ring(s0, "y", 4, 1)
    u2 = jnp.concatenate([u1, ring(u1, "xl", 2, 1)])
    up, um = ring(u2, "y", 4, 3), ring(u2, "y", 4, 1)
    s2a, s2b = ring(sp[:72], "y", 4, 3), ring(sm[72:], "y", 4, 1)
    ut = ring(up, "y", 4, 3)
    far_other = swap_cores(far)
    u = jnp.concatenate([u2, up, ut, um])
    offsets = [
        (((y + dy) % 4 * 2 + (xl + dx) % 2) * 2 + (core + dc) % 2) * 16
        for dy in range(4)
        for dx in range(2)
        for dc in range(2)
    ]
    at = jnp.stack([y] + offsets).astype(jnp.int32)
    squares, linear = moments(at, own, other, far, far_other, s0, sp, sm, s2a, s2b, u)

    sums = jnp.stack([squares, linear]).astype(BF16).reshape(2, 4, 144, 256)
    sums = lax.all_to_all(sums.transpose(1, 0, 2, 3), "y", 0, 0, tiled=True)
    sums = jnp.sum(sums.astype(F32), axis=0).reshape(288, 256).T
    sums = lax.all_to_all(sums, ("z", "xh"), 0, 0, tiled=True)
    sums = jnp.sum(sums.reshape(16, 16, 288), axis=0)
    side = inputs.shape[1]
    return (
        sums[:, :144] * (1.0 / (side * side * examples)),
        sums[:, 144:] * (1.0 / (side * math.sqrt(examples))),
    )


def solution(mesh):
    fine = Mesh(mesh.devices.reshape(SIZES), AXES)
    every, columns = ("z", "xh", "y", "xl", "c"), ("y", "xl", "c")
    return jax.shard_map(
        on_device,
        mesh=fine,
        in_specs=(P(every), P(every), P(None, columns), P(None, columns)),
        out_specs=(P(("z", "xh"), columns), P(("z", "xh"), columns)),
        check_vma=False,
    )
```

```python
import functools
import math

import jax
import jax.numpy as jnp
from jax import lax
from jax.experimental import pallas as pl
from jax.experimental.pallas import tpu as pltpu
from jax.sharding import Mesh, PartitionSpec as P

AXES = ("z", "xh", "y", "xl", "c")
SIZES = (8, 2, 4, 2, 2)
BF16 = jnp.bfloat16
F32 = jnp.float32
CONTRACT_LAST = (((1,), (1,)), ((), ()))


def ring(value, axis, size, step):
    return lax.ppermute(value, axis, [(i, (i + step) % size) for i in range(size)])


def swap_cores(value):
    return lax.ppermute(value, "c", [(0, 1), (1, 0)])


def swap_x(value):
    def partner(x, core):
        return (x + 1 if (x + core) % 2 == 0 else x - 1) % 4

    pairs = [(x * 2 + core, partner(x, core) * 2 + core) for x in range(4) for core in range(2)]
    return lax.ppermute(value, ("xh", "xl", "c"), pairs)


def prepare(inputs, out_grads):
    both = jnp.stack([inputs, out_grads])
    padded = jnp.pad(both, ((0, 0), (0, 0), (0, 0), (0, 2), (0, 0)))
    return padded.reshape(2, inputs.shape[0], 224, 256)


def moments_kernel(
    at_ref, own, other, far, far_other, a0, b0, ap, bp, am, bm, a2, b2, u_near, u_core,
    squares_ref, linear_ref, basis, rows, patches, grads, out_basis,
):
    y = at_ref[0]

    for step, top, bottom in ((0, a0, b0), (1, ap, bp), (3, am, bm), (2, a2, b2)):
        owner = lax.rem(y + step, 4)
        at = pl.multiple_of((owner % 2) * 144, 16)
        basis[owner // 2, pl.ds(at, 80), :] = top[...]
        basis[owner // 2, pl.ds(pl.multiple_of(at + 80, 16), 64), :] = bottom[0:64, :]
    for piece in range(16):
        source = u_near if piece < 8 else u_core
        row = pl.multiple_of(at_ref[1 + piece], 16)
        out_basis[pl.ds(row, 16), :] = source[16 * (piece % 8) : 16 * (piece % 8) + 16, :]
    rows[...] = jnp.zeros_like(rows)
    grads[...] = jnp.zeros_like(grads)
    squares_ref[...] = jnp.zeros_like(squares_ref)
    linear_ref[...] = jnp.zeros_like(linear_ref)

    for group in (own, other, far, far_other):
        for n in range(4):
            feature = group[0, n].astype(F32)
            rows[n, 0, 16:240, :] = pltpu.roll(feature, 1, 0).astype(BF16)
            rows[n, 1, 16:240, :] = group[0, n]
            rows[n, 2, 16:240, :] = pltpu.roll(feature, 223, 0).astype(BF16)
            at = slice(256 * n, 256 * n + 256)
            for tap in range(9):
                ky, kx = tap // 3, tap % 3
                shifted = rows[n, kx, 16 * ky : 16 * ky + 256, :]
                if tap < 4:
                    patches[0, at, 256 * tap : 256 * tap + 256] = shifted
                elif tap == 4:
                    patches[0, at, 1024:1152] = shifted[:, :128]
                    patches[1, at, 0:128] = shifted[:, 128:]
                else:
                    patches[1, at, 256 * tap - 1152 : 256 * tap - 896] = shifted
            grads[n, 0:224, :] = lax.dot_general(
                group[1, n], out_basis[...], CONTRACT_LAST, preferred_element_type=F32
            ).astype(BF16)
        for block in range(2):
            rotated = lax.dot_general(
                basis[block], patches[block], CONTRACT_LAST, preferred_element_type=F32
            ).astype(BF16)
            squares, linear = squares_ref[block], linear_ref[block]
            for n in range(4):
                projected = jnp.dot(
                    rotated[:, 256 * n : 256 * n + 256], grads[n], preferred_element_type=F32
                )
                squares = squares + projected * projected
                linear = linear + projected
            squares_ref[block] = squares
            linear_ref[block] = linear


def moments(at, *operands):
    shape = jax.ShapeDtypeStruct((2, 288, 256), F32)
    vmem = pl.BlockSpec(memory_space=pltpu.VMEM)
    return pl.pallas_call(
        moments_kernel,
        out_shape=(shape, shape),
        in_specs=[pl.BlockSpec(memory_space=pltpu.SMEM)] + [vmem] * len(operands),
        out_specs=(vmem, vmem),
        scratch_shapes=[
            pltpu.VMEM((2, 288, 1152), BF16),
            pltpu.VMEM((4, 3, 288, 256), BF16),
            pltpu.VMEM((2, 1024, 1152), BF16),
            pltpu.VMEM((4, 256, 256), BF16),
            pltpu.VMEM((256, 256), BF16),
        ],
        compiler_params=pltpu.CompilerParams(vmem_limit_bytes=40 * 2**20),
        name="moments",
    )(at, *operands)


def on_device(inputs, out_grads, patch_basis, output_basis):
    examples = inputs.shape[0] * math.prod(SIZES)
    y, xl, core = lax.axis_index("y"), lax.axis_index("xl"), lax.axis_index("c")

    shard = jnp.concatenate(
        [patch_basis.T, jnp.pad(output_basis.T, ((0, 0), (0, 1152 - 256)))]
    )
    a0, b0 = shard[:80], shard[80:]
    ap, am = ring(a0, "y", 4, 3), ring(a0, "y", 4, 1)
    bp, bm = ring(b0, "y", 4, 3), ring(b0, "y", 4, 1)
    a2, b2 = ring(ap, "y", 4, 3), ring(bm, "y", 4, 1)
    own = prepare(inputs, out_grads)
    other = swap_cores(own)
    far = swap_x(own)
    far_other = swap_cores(far)
    u_ring = jnp.concatenate([piece[64:, :256] for piece in (b0, bp, b2, bm)])
    u_near = jnp.concatenate([u_ring, ring(u_ring, "xl", 2, 1)])
    u_core = swap_cores(u_near)
    offsets = [
        (((y + dy) % 4 * 2 + (xl + dx) % 2) * 2 + (core + dc) % 2) * 16
        for dc in range(2)
        for dx in range(2)
        for dy in range(4)
    ]
    at = jnp.stack([y] + offsets).astype(jnp.int32)
    squares, linear = moments(
        at, own, other, far, far_other, a0, b0, ap, bp, am, bm, a2, b2, u_near, u_core
    )

    sums = jnp.stack([squares, linear]).astype(BF16).reshape(2, 4, 144, 256)
    sums = lax.all_to_all(sums.transpose(1, 0, 2, 3), "y", 0, 0, tiled=True)
    sums = jnp.sum(sums.astype(F32), axis=0).reshape(288, 256).T
    sums = lax.all_to_all(sums, ("z", "xh"), 0, 0, tiled=True)
    sums = jnp.sum(sums.reshape(16, 16, 288), axis=0)
    side = inputs.shape[1]
    return (
        sums[:, :144] * (1.0 / (side * side * examples)),
        sums[:, 144:] * (1.0 / (side * math.sqrt(examples))),
    )


def solution(mesh):
    fine = Mesh(mesh.devices.reshape(SIZES), AXES)
    every, columns = ("z", "xh", "y", "xl", "c"), ("y", "xl", "c")
    return jax.shard_map(
        on_device,
        mesh=fine,
        in_specs=(P(every), P(every), P(None, columns), P(None, columns)),
        out_specs=(P(("z", "xh"), columns), P(("z", "xh"), columns)),
        check_vma=False,
    )
```

```python
import math

import jax
import jax.numpy as jnp
from jax import lax
from jax.experimental import pallas as pl
from jax.experimental.pallas import tpu as pltpu
from jax.sharding import Mesh, PartitionSpec as P

AXES = ("z", "xh", "y", "xl", "c")
SIZES = (8, 2, 4, 2, 2)
BF16 = jnp.bfloat16
F32 = jnp.float32
CONTRACT_LAST = (((1,), (1,)), ((), ()))
TOP = 80


def ring(value, axis, size, step):
    return lax.ppermute(value, axis, [(i, (i + step) % size) for i in range(size)])


def swap_cores(value):
    return lax.ppermute(value, "c", [(0, 1), (1, 0)])


def swap_x(value, turn):
    def partner(x, core):
        return (x + 1 if (x + core + turn) % 2 == 0 else x - 1) % 4

    pairs = [(x * 2 + core, partner(x, core) * 2 + core) for x in range(4) for core in range(2)]
    return lax.ppermute(value, ("xh", "xl", "c"), pairs)


def prepare(inputs, out_grads):
    both = jnp.stack([inputs, out_grads])
    padded = jnp.pad(both, ((0, 0), (0, 0), (0, 0), (0, 2), (0, 0)))
    return padded.reshape(2, inputs.shape[0], 224, 256)


def clear(rows, grads):
    rows[...] = jnp.zeros_like(rows)
    grads[...] = jnp.zeros_like(grads)


def add_group(group, basis, out_basis, squares_ref, linear_ref, rows, patches, grads):
    for n in range(4):
        feature = group[0, n].astype(F32)
        rows[n, 0, 16:240, :] = pltpu.roll(feature, 1, 0).astype(BF16)
        rows[n, 1, 16:240, :] = group[0, n]
        rows[n, 2, 16:240, :] = pltpu.roll(feature, 223, 0).astype(BF16)
        at = slice(256 * n, 256 * n + 256)
        for tap in range(9):
            ky, kx = tap // 3, tap % 3
            shifted = rows[n, kx, 16 * ky : 16 * ky + 256, :]
            if tap < 4:
                patches[0, at, 256 * tap : 256 * tap + 256] = shifted
            elif tap == 4:
                patches[0, at, 1024:1152] = shifted[:, :128]
                patches[1, at, 0:128] = shifted[:, 128:]
            else:
                patches[1, at, 256 * tap - 1152 : 256 * tap - 896] = shifted
        grads[n, 0:224, :] = lax.dot_general(
            group[1, n], out_basis[...], CONTRACT_LAST, preferred_element_type=F32
        ).astype(BF16)
    for block in range(2):
        rotated = lax.dot_general(
            basis[block], patches[block], CONTRACT_LAST, preferred_element_type=F32
        ).astype(BF16)
        squares, linear = squares_ref[block], linear_ref[block]
        for n in range(4):
            projected = jnp.dot(
                rotated[:, 256 * n : 256 * n + 256], grads[n], preferred_element_type=F32
            )
            squares = squares + projected * projected
            linear = linear + projected
        squares_ref[block] = squares
        linear_ref[block] = linear


def near_kernel(
    own, other, here, plus, minus, two_top, two_bottom,
    u_here, u_two,
    squares_ref, linear_ref, basis, out_basis, rows, patches, grads,
):
    y, xl, core = lax.axis_index("y"), lax.axis_index("xl"), lax.axis_index("c")

    def at(step, first, count):
        owner = lax.rem(y + step, 4)
        start = pl.multiple_of((owner % 2) * 144 + first, 16)
        return owner // 2, pl.ds(start, count), slice(None)

    basis[at(0, 0, 144)] = here[...]
    basis[at(1, 0, 144)] = plus[...]
    basis[at(3, 0, 144)] = minus[...]
    basis[at(2, 0, TOP)] = two_top[0:TOP, :]
    basis[at(2, TOP, 144 - TOP)] = two_bottom[0 : 144 - TOP, :]
    for dy, (source, row) in enumerate(
        ((u_here, 0), (two_top, TOP), (u_two, 0), (two_bottom, 144 - TOP))
    ):
        for piece in range(4):
            dx, dc = piece // 2, piece % 2
            owner = (lax.rem(y + dy, 4) * 2 + lax.rem(xl + dx, 2)) * 2 + lax.rem(core + dc, 2)
            place = owner % 2 * 128 + owner // 2 * 16
            out_basis[pl.ds(pl.multiple_of(place, 16), 16), :] = source[
                row : row + 16, 256 * piece : 256 * piece + 256
            ]
    clear(rows, grads)
    squares_ref[...] = jnp.zeros_like(squares_ref)
    linear_ref[...] = jnp.zeros_like(linear_ref)
    for group in (own, other):
        add_group(group, basis, out_basis, squares_ref, linear_ref, rows, patches, grads)


def far_kernel(
    far, far_other, squares_in, linear_in, basis, out_basis,
    sums, squares_ref, linear_ref, rows, patches, grads,
):
    clear(rows, grads)
    squares_ref[...] = squares_in[...]
    linear_ref[...] = linear_in[...]
    for group in (far, far_other):
        add_group(group, basis, out_basis, squares_ref, linear_ref, rows, patches, grads)
    for owner in range(4):
        at = slice(144 * (owner % 2), 144 * (owner % 2) + 144)
        for half in range(2):
            lanes = slice(128 * half, 128 * half + 128)
            sums[4 * half + owner, 0] = squares_ref[owner // 2, at, lanes].astype(BF16)
            sums[4 * half + owner, 1] = linear_ref[owner // 2, at, lanes].astype(BF16)


def call(kernel, name, out_shape, scratch, *operands):
    vmem = pl.BlockSpec(memory_space=pltpu.VMEM)
    work = [
        pltpu.VMEM((4, 3, 288, 256), BF16),
        pltpu.VMEM((2, 1024, 1152), BF16),
        pltpu.VMEM((4, 256, 256), BF16),
    ]
    return pl.pallas_call(
        kernel,
        out_shape=out_shape,
        in_specs=[vmem] * len(operands),
        out_specs=jax.tree.map(lambda _: vmem, out_shape),
        scratch_shapes=scratch + work,
        compiler_params=pltpu.CompilerParams(vmem_limit_bytes=20 * 2**20),
        cost_estimate=pl.CostEstimate(flops=4 * 10**9, bytes_accessed=10**6, transcendentals=0),
        name=name,
    )(*operands)


def on_device(inputs, out_grads, patch_basis, output_basis):
    examples = inputs.shape[0] * math.prod(SIZES)
    side = inputs.shape[1]

    shard = patch_basis.T
    plus, minus = ring(shard, "y", 4, 3), ring(shard, "y", 4, 1)
    u0 = output_basis.T
    u1 = jnp.concatenate([u0, swap_cores(u0)], axis=1)
    u2 = jnp.concatenate([u1, swap_x(u1, 1)], axis=1)
    plus, minus, u2 = lax.optimization_barrier((plus, minus, u2))
    tail = jnp.pad(u2, ((0, 0), (0, 128)))
    two_top = ring(jnp.concatenate([plus[:TOP], tail]), "y", 4, 3)
    two_bottom = ring(jnp.concatenate([minus[TOP:], tail]), "y", 4, 1)
    u_two = ring(u2, "y", 4, 2)
    own = prepare(inputs, out_grads)
    other = swap_cores(own)
    far = swap_x(own, 0)
    far, two_top, two_bottom, u_two = lax.optimization_barrier(
        (far, two_top, two_bottom, u_two)
    )
    far_other = swap_cores(far)

    moment = jax.ShapeDtypeStruct((2, 288, 256), F32)
    squares, linear, basis, out_basis = call(
        near_kernel,
        "near_examples",
        (
            moment,
            moment,
            jax.ShapeDtypeStruct((2, 288, 1152), BF16),
            jax.ShapeDtypeStruct((256, 256), BF16),
        ),
        [],
        own, other, shard, plus, minus, two_top, two_bottom,
        u2, u_two,
    )
    sums = call(
        far_kernel,
        "far_examples",
        jax.ShapeDtypeStruct((8, 2, 144, 128), BF16),
        [pltpu.VMEM((2, 288, 256), F32)] * 2,
        far, far_other, squares, linear, basis, out_basis,
    )

    sums = lax.all_to_all(sums, ("xh", "y"), 0, 0, tiled=True)
    sums = jnp.sum(sums.astype(F32), axis=0).reshape(288, 128).T
    sums = lax.all_to_all(sums, "z", 0, 0, tiled=True)
    sums = jnp.sum(sums.reshape(8, 16, 288), axis=0)
    return (
        sums[:, :144] * (1.0 / (side * side * examples)),
        sums[:, 144:] * (1.0 / (side * math.sqrt(examples))),
    )


def solution(mesh):
    fine = Mesh(mesh.devices.reshape(SIZES), AXES)
    every, columns = ("z", "xh", "y", "xl", "c"), ("y", "xl", "c")
    return jax.shard_map(
        on_device,
        mesh=fine,
        in_specs=(P(every), P(every), P(None, columns), P(None, columns)),
        out_specs=(P(("z", "xh"), columns), P(("z", "xh"), columns)),
        check_vma=False,
    )
```

```python
import math

import jax
import jax.numpy as jnp
from jax import lax
from jax.experimental import pallas as pl
from jax.experimental.pallas import tpu as pltpu
from jax.sharding import Mesh, PartitionSpec as P

AXES = ("zh", "zl", "xh", "y", "xl", "c")
SIZES = (4, 2, 2, 4, 2, 2)
BF16 = jnp.bfloat16
F32 = jnp.float32
CONTRACT_LAST = (((1,), (1,)), ((), ()))
TOP = 80


def ring(value, axis, size, step):
    return lax.ppermute(value, axis, [(i, (i + step) % size) for i in range(size)])


def swap_cores(value):
    return lax.ppermute(value, "c", [(0, 1), (1, 0)])


def swap_x(value, turn):
    def partner(x, core):
        return (x + 1 if (x + core + turn) % 2 == 0 else x - 1) % 4

    pairs = [(x * 2 + core, partner(x, core) * 2 + core) for x in range(4) for core in range(2)]
    return lax.ppermute(value, ("xh", "xl", "c"), pairs)


def prepare(inputs, out_grads):
    both = jnp.stack([inputs, out_grads])
    padded = jnp.pad(both, ((0, 0), (0, 0), (0, 0), (0, 2), (0, 0)))
    return padded.reshape(2, inputs.shape[0], 224, 256)


def clear(rows, grads):
    rows[:, :, 0:16, :] = jnp.zeros((4, 3, 16, 256), BF16)
    rows[:, :, 240:288, :] = jnp.zeros((4, 3, 48, 256), BF16)
    grads[:, 224:256, :] = jnp.zeros((4, 32, 256), BF16)


def add_group(group, basis, out_basis, squares_ref, linear_ref, rows, patches, grads):
    for n in range(4):
        feature = group[0, n].astype(F32)
        rows[n, 0, 16:240, :] = pltpu.roll(feature, 1, 0).astype(BF16)
        rows[n, 1, 16:240, :] = group[0, n]
        rows[n, 2, 16:240, :] = pltpu.roll(feature, 223, 0).astype(BF16)
        at = slice(256 * n, 256 * n + 256)
        for tap in range(9):
            ky, kx = tap // 3, tap % 3
            shifted = rows[n, kx, 16 * ky : 16 * ky + 256, :]
            if tap < 4:
                patches[0, at, 256 * tap : 256 * tap + 256] = shifted
            elif tap == 4:
                patches[0, at, 1024:1152] = shifted[:, :128]
                patches[1, at, 0:128] = shifted[:, 128:]
            else:
                patches[1, at, 256 * tap - 1152 : 256 * tap - 896] = shifted
        grads[n, 0:224, :] = lax.dot_general(
            group[1, n], out_basis[...], CONTRACT_LAST, preferred_element_type=F32
        ).astype(BF16)
    for block in range(2):
        rotated = lax.dot_general(
            basis[block], patches[block], CONTRACT_LAST, preferred_element_type=F32
        ).astype(BF16)
        squares, linear = squares_ref[block], linear_ref[block]
        for n in range(4):
            projected = jnp.dot(
                rotated[:, 256 * n : 256 * n + 256], grads[n], preferred_element_type=F32
            )
            squares = squares + projected * projected
            linear = linear + projected
        squares_ref[block] = squares
        linear_ref[block] = linear


def near_kernel(
    own, other, here, plus, minus, two_top, two_bottom,
    u_here, u_two,
    squares_ref, linear_ref, basis, out_basis, rows, patches, grads,
):
    y, xl, core = lax.axis_index("y"), lax.axis_index("xl"), lax.axis_index("c")

    def at(step, first, count):
        owner = lax.rem(y + step, 4)
        start = pl.multiple_of((owner % 2) * 144 + first, 16)
        return owner // 2, pl.ds(start, count), slice(None)

    basis[at(0, 0, 144)] = here[...]
    basis[at(1, 0, 144)] = plus[...]
    basis[at(3, 0, 144)] = minus[...]
    basis[at(2, 0, TOP)] = two_top[0:TOP, :]
    basis[at(2, TOP, 144 - TOP)] = two_bottom[0 : 144 - TOP, :]
    for dy, (source, row) in enumerate(
        ((u_here, 0), (two_top, TOP), (u_two, 0), (two_bottom, 144 - TOP))
    ):
        for piece in range(4):
            dx, dc = piece // 2, piece % 2
            owner = (lax.rem(y + dy, 4) * 2 + lax.rem(xl + dx, 2)) * 2 + lax.rem(core + dc, 2)
            place = owner % 2 * 128 + owner // 2 * 16
            out_basis[pl.ds(pl.multiple_of(place, 16), 16), :] = source[
                row : row + 16, 256 * piece : 256 * piece + 256
            ]
    clear(rows, grads)
    squares_ref[...] = jnp.zeros_like(squares_ref)
    linear_ref[...] = jnp.zeros_like(linear_ref)
    for group in (own, other):
        add_group(group, basis, out_basis, squares_ref, linear_ref, rows, patches, grads)


def far_kernel(
    far, far_other, squares_in, linear_in, basis, out_basis,
    sums, squares_ref, linear_ref, rows, patches, grads,
):
    clear(rows, grads)
    squares_ref[...] = squares_in[...]
    linear_ref[...] = linear_in[...]
    for group in (far, far_other):
        add_group(group, basis, out_basis, squares_ref, linear_ref, rows, patches, grads)
    for owner in range(4):
        at = slice(144 * (owner % 2), 144 * (owner % 2) + 144)
        for half in range(2):
            lanes = slice(128 * half, 128 * half + 128)
            sums[4 * half + owner, 0] = squares_ref[owner // 2, at, lanes].astype(BF16)
            sums[4 * half + owner, 1] = linear_ref[owner // 2, at, lanes].astype(BF16)


def call(kernel, name, out_shape, scratch, *operands):
    vmem = pl.BlockSpec(memory_space=pltpu.VMEM)
    work = [
        pltpu.VMEM((4, 3, 288, 256), BF16),
        pltpu.VMEM((2, 1024, 1152), BF16),
        pltpu.VMEM((4, 256, 256), BF16),
    ]
    return pl.pallas_call(
        kernel,
        out_shape=out_shape,
        in_specs=[vmem] * len(operands),
        out_specs=jax.tree.map(lambda _: vmem, out_shape),
        scratch_shapes=scratch + work,
        compiler_params=pltpu.CompilerParams(vmem_limit_bytes=20 * 2**20),
        cost_estimate=pl.CostEstimate(flops=4 * 10**9, bytes_accessed=10**6, transcendentals=0),
        name=name,
    )(*operands)


def on_device(inputs, out_grads, patch_basis, output_basis):
    examples = inputs.shape[0] * math.prod(SIZES)
    side = inputs.shape[1]

    shard = patch_basis.T
    plus, minus = ring(shard, "y", 4, 3), ring(shard, "y", 4, 1)
    u0 = output_basis.T
    u1 = jnp.concatenate([u0, swap_cores(u0)], axis=1)
    u2 = jnp.concatenate([u1, swap_x(u1, 1)], axis=1)
    plus, minus, u2 = lax.optimization_barrier((plus, minus, u2))
    tail = jnp.pad(u2, ((0, 0), (0, 128)))
    two_top = ring(jnp.concatenate([plus[:TOP], tail]), "y", 4, 3)
    two_bottom = ring(jnp.concatenate([minus[TOP:], tail]), "y", 4, 1)
    u_two = ring(u2, "y", 4, 2)
    own = prepare(inputs, out_grads)
    other = swap_cores(own)
    far = swap_x(own, 0)
    far, two_top, two_bottom, u_two = lax.optimization_barrier(
        (far, two_top, two_bottom, u_two)
    )
    far_other = swap_cores(far)

    moment = jax.ShapeDtypeStruct((2, 288, 256), F32)
    squares, linear, basis, out_basis = call(
        near_kernel,
        "near_examples",
        (
            moment,
            moment,
            jax.ShapeDtypeStruct((2, 288, 1152), BF16),
            jax.ShapeDtypeStruct((256, 256), BF16),
        ),
        [],
        own, other, shard, plus, minus, two_top, two_bottom,
        u2, u_two,
    )
    sums = call(
        far_kernel,
        "far_examples",
        jax.ShapeDtypeStruct((8, 2, 144, 128), BF16),
        [pltpu.VMEM((2, 288, 256), F32)] * 2,
        far, far_other, squares, linear, basis, out_basis,
    )

    sums = lax.all_to_all(sums, ("xh", "y"), 0, 0, tiled=True)
    sums = jnp.sum(sums.astype(F32), axis=0).reshape(288, 128).T.astype(BF16)
    sums = lax.all_to_all(sums, ("zh", "zl"), 0, 0, tiled=True)
    sums = jnp.sum(sums.reshape(8, 16, 288).astype(F32), axis=0)
    return (
        sums[:, :144] * (1.0 / (side * side * examples)),
        sums[:, 144:] * (1.0 / (side * math.sqrt(examples))),
    )


def solution(mesh):
    fine = Mesh(mesh.devices.reshape(SIZES), AXES)
    every, columns, rows = AXES, AXES[3:], AXES[:3]
    return jax.shard_map(
        on_device,
        mesh=fine,
        in_specs=(P(every), P(every), P(None, columns), P(None, columns)),
        out_specs=(P(rows, columns), P(rows, columns)),
        check_vma=False,
    )
```

```python
import math

import jax
import jax.numpy as jnp
from jax import lax
from jax.experimental import pallas as pl
from jax.experimental.pallas import tpu as pltpu
from jax.sharding import Mesh, PartitionSpec as P

AXES = ("zh", "zl", "xh", "y", "xl", "c")
SIZES = (4, 2, 2, 4, 2, 2)
BF16 = jnp.bfloat16
F32 = jnp.float32
CONTRACT_LAST = (((1,), (1,)), ((), ()))
TOP = 80


def ring(value, axis, size, step):
    return lax.ppermute(value, axis, [(i, (i + step) % size) for i in range(size)])


def swap_cores(value):
    return lax.ppermute(value, "c", [(0, 1), (1, 0)])


def swap_x(value, turn):
    def partner(x, core):
        return (x + 1 if (x + core + turn) % 2 == 0 else x - 1) % 4

    pairs = [(x * 2 + core, partner(x, core) * 2 + core) for x in range(4) for core in range(2)]
    return lax.ppermute(value, ("xh", "xl", "c"), pairs)


def prepare(inputs, out_grads):
    both = jnp.stack([inputs, out_grads])
    padded = jnp.pad(both, ((0, 0), (0, 0), (0, 0), (0, 2), (0, 0)))
    return padded.reshape(2, inputs.shape[0], 224, 256)


def take_patches(group, rows, patches, blocks):
    for n in range(4):
        feature = group[0, n].astype(F32)
        rows[n, 0, 16:240, :] = pltpu.roll(feature, 1, 0).astype(BF16)
        rows[n, 1, 16:240, :] = group[0, n]
        rows[n, 2, 16:240, :] = pltpu.roll(feature, 223, 0).astype(BF16)
        at = slice(256 * n, 256 * n + 256)
        for tap in range(9):
            ky, kx = tap // 3, tap % 3
            shifted = rows[n, kx, 16 * ky : 16 * ky + 256, :]
            if tap <= 4 and 0 in blocks:
                last = min(256 * tap + 256, 1152)
                patches[0, at, 256 * tap : last] = shifted[:, : last - 256 * tap]
            if tap >= 4 and 1 in blocks:
                first = max(256 * tap - 1152, 0)
                patches[1, at, first : 256 * tap - 896] = shifted[:, first + 1152 - 256 * tap :]


def clear_edges(rows):
    rows[:, :, 0:16, :] = jnp.zeros((4, 3, 16, 256), BF16)
    rows[:, :, 240:288, :] = jnp.zeros((4, 3, 48, 256), BF16)


def rotate(basis, patches):
    return lax.dot_general(
        basis, patches, CONTRACT_LAST, preferred_element_type=F32
    ).astype(BF16)


def rotate_grads(group, out_basis, grads):
    for n in range(4):
        grads[n, 0:224, :] = lax.dot_general(
            group[1, n], out_basis[...], CONTRACT_LAST, preferred_element_type=F32
        ).astype(BF16)


def add_moments(rotated, grads, squares_ref, linear_ref, block):
    squares, linear = squares_ref[block], linear_ref[block]
    for n in range(4):
        projected = jnp.dot(
            rotated[:, 256 * n : 256 * n + 256], grads[n], preferred_element_type=F32
        )
        squares = squares + projected * projected
        linear = linear + projected
    squares_ref[block] = squares
    linear_ref[block] = linear


def first_kernel(own, other, here, plus, minus, rotated, basis, rows, patches):
    y = lax.axis_index("y")
    odd = lax.rem(y, 2)
    basis[pl.ds(pl.multiple_of(odd * 144, 16), 144), :] = here[...]
    basis[pl.ds(pl.multiple_of(144 - odd * 144, 16), 144), :] = jnp.where(
        odd == 0, plus[...], minus[...]
    )
    clear_edges(rows)
    for block in range(2):

        @pl.when(y // 2 == block)
        def _(block=block):
            for at, group in enumerate((own, other)):
                take_patches(group, rows, patches, (block,))
                rotated[at] = rotate(basis[...], patches[block])


def near_kernel(
    own, other, rotated, first, plus, minus, two_top, two_bottom, u_here, u_two,
    squares_ref, linear_ref, basis, out_basis, rows, patches, grads,
):
    y, xl, core = lax.axis_index("y"), lax.axis_index("xl"), lax.axis_index("c")
    odd, own_block = lax.rem(y, 2), y // 2
    at = odd * 144
    basis[own_block] = first[...]
    second = basis.at[1 - own_block]
    second[pl.ds(pl.multiple_of(at, 16), TOP), :] = two_top[0:TOP, :]
    second[pl.ds(pl.multiple_of(at + TOP, 16), 144 - TOP), :] = two_bottom[0 : 144 - TOP, :]
    second[pl.ds(pl.multiple_of(144 - at, 16), 144), :] = jnp.where(
        odd == 0, minus[...], plus[...]
    )
    for dy, (source, row) in enumerate(
        ((u_here, 0), (two_top, TOP), (u_two, 0), (two_bottom, 144 - TOP))
    ):
        for piece in range(4):
            dc, dx = piece // 2, piece % 2
            owner = (lax.rem(y + dy, 4) * 2 + lax.rem(xl + dx, 2)) * 2 + lax.rem(core + dc, 2)
            place = owner % 2 * 128 + owner // 2 * 16
            out_basis[pl.ds(pl.multiple_of(place, 16), 16), :] = source[
                row : row + 16, 256 * piece : 256 * piece + 256
            ]
    clear_edges(rows)
    grads[:, 224:256, :] = jnp.zeros((4, 32, 256), BF16)
    squares_ref[...] = jnp.zeros_like(squares_ref)
    linear_ref[...] = jnp.zeros_like(linear_ref)
    for block in range(2):

        @pl.when(own_block == block)
        def _(block=block):
            for n, group in enumerate((own, other)):
                take_patches(group, rows, patches, (1 - block,))
                rotate_grads(group, out_basis, grads)
                add_moments(rotated[n], grads, squares_ref, linear_ref, block)
                add_moments(
                    rotate(basis[1 - block], patches[1 - block]),
                    grads, squares_ref, linear_ref, 1 - block,
                )


def far_kernel(
    far, far_other, squares_in, linear_in, basis, out_basis,
    sums, squares_ref, linear_ref, rows, patches, grads,
):
    clear_edges(rows)
    grads[:, 224:256, :] = jnp.zeros((4, 32, 256), BF16)
    squares_ref[...] = squares_in[...]
    linear_ref[...] = linear_in[...]
    for group in (far, far_other):
        take_patches(group, rows, patches, (0, 1))
        rotate_grads(group, out_basis, grads)
        for block in range(2):
            add_moments(
                rotate(basis[block], patches[block]), grads, squares_ref, linear_ref, block
            )
    for owner in range(4):
        at = slice(144 * (owner % 2), 144 * (owner % 2) + 144)
        for half in range(2):
            lanes = slice(128 * half, 128 * half + 128)
            sums[4 * half + owner, 0] = squares_ref[owner // 2, at, lanes].astype(BF16)
            sums[4 * half + owner, 1] = linear_ref[owner // 2, at, lanes].astype(BF16)


def call(kernel, name, flops, out_shape, scratch, *operands):
    vmem = pl.BlockSpec(memory_space=pltpu.VMEM)
    return pl.pallas_call(
        kernel,
        out_shape=out_shape,
        in_specs=[vmem] * len(operands),
        out_specs=jax.tree.map(lambda _: vmem, out_shape),
        scratch_shapes=scratch,
        compiler_params=pltpu.CompilerParams(vmem_limit_bytes=20 * 2**20),
        cost_estimate=pl.CostEstimate(flops=flops, bytes_accessed=10**6, transcendentals=0),
        name=name,
    )(*operands)


def forward_kernel(plus, minus, eigenvectors, top, bottom):
    top[0:TOP, :] = plus[0:TOP, :]
    bottom[0 : 144 - TOP, :] = minus[TOP:144, :]
    for target, row in ((top, TOP), (bottom, 144 - TOP)):
        target[row : row + 16, 0:1024] = eigenvectors[...]
        target[row : row + 16, 1024:1152] = jnp.zeros((16, 128), BF16)


def on_device(inputs, out_grads, patch_basis, output_basis):
    examples = inputs.shape[0] * math.prod(SIZES)
    side = inputs.shape[1]

    shard = patch_basis.T
    plus, minus = ring(shard, "y", 4, 3), ring(shard, "y", 4, 1)
    u0 = output_basis.T
    u1 = jnp.concatenate([u0, swap_x(u0, 0)], axis=1)
    u2 = jnp.concatenate([u1, swap_cores(u1)], axis=1)
    top, bottom = call(
        forward_kernel,
        "forward",
        20*10**9,
        tuple(jax.ShapeDtypeStruct((n + 16, 1152), BF16) for n in (TOP, 144 - TOP)),
        [],
        plus, minus, u2,
    )
    two_top, two_bottom = ring(top, "y", 4, 3), ring(bottom, "y", 4, 1)
    u_two = ring(u2, "y", 4, 2)
    own = prepare(inputs, out_grads)
    other = swap_cores(own)
    far = swap_x(own, 0)

    moment = jax.ShapeDtypeStruct((2, 288, 256), F32)
    rows, patches = pltpu.VMEM((4, 3, 288, 256), BF16), pltpu.VMEM((2, 1024, 1152), BF16)
    grads = pltpu.VMEM((4, 256, 256), BF16)
    rotated, first = call(
        first_kernel,
        "first_block_near",
        4*10**9,
        (
            jax.ShapeDtypeStruct((2, 288, 1024), BF16),
            jax.ShapeDtypeStruct((288, 1152), BF16),
        ),
        [rows, patches],
        own, other, shard, plus, minus,
    )
    far, two_top, two_bottom, u_two, rotated = lax.optimization_barrier(
        (far, two_top, two_bottom, u_two, rotated)
    )
    far_other = swap_cores(far)
    squares, linear, basis, out_basis = call(
        near_kernel,
        "near_examples",
        4 * 10**9,
        (
            moment,
            moment,
            jax.ShapeDtypeStruct((2, 288, 1152), BF16),
            jax.ShapeDtypeStruct((256, 256), BF16),
        ),
        [rows, patches, grads],
        own, other, rotated, first, plus, minus, two_top, two_bottom, u2, u_two,
    )
    sums = call(
        far_kernel,
        "far_examples",
        4 * 10**9,
        jax.ShapeDtypeStruct((8, 2, 144, 128), BF16),
        [pltpu.VMEM((2, 288, 256), F32)] * 2 + [rows, patches, grads],
        far, far_other, squares, linear, basis, out_basis,
    )

    sums = lax.all_to_all(sums, ("xh", "y"), 0, 0, tiled=True)
    sums = jnp.sum(sums.astype(F32), axis=0).reshape(288, 128).T.astype(BF16)
    sums = lax.all_to_all(sums, ("zh", "zl"), 0, 0, tiled=True)
    sums = jnp.sum(sums.reshape(8, 16, 288).astype(F32), axis=0)
    return (
        sums[:, :144] * (1.0 / (side * side * examples)),
        sums[:, 144:] * (1.0 / (side * math.sqrt(examples))),
    )


def solution(mesh):
    fine = Mesh(mesh.devices.reshape(SIZES), AXES)
    every, columns, rows = AXES, AXES[3:], AXES[:3]
    return jax.shard_map(
        on_device,
        mesh=fine,
        in_specs=(P(every), P(every), P(None, columns), P(None, columns)),
        out_specs=(P(rows, columns), P(rows, columns)),
        check_vma=False,
    )
```

```python
import math

import jax
import jax.numpy as jnp
from jax import lax
from jax.experimental import pallas as pl
from jax.experimental.pallas import tpu as pltpu
from jax.sharding import Mesh, PartitionSpec as P

AXES = ("zh", "zl", "xh", "y", "xl", "c")
SIZES = (4, 2, 2, 4, 2, 2)
BF16 = jnp.bfloat16
F32 = jnp.float32
CONTRACT_LAST = (((1,), (1,)), ((), ()))
TOP = 80


def ring(value, axis, size, step):
    return lax.ppermute(value, axis, [(i, (i + step) % size) for i in range(size)])


def swap_cores(value):
    return lax.ppermute(value, "c", [(0, 1), (1, 0)])


def swap_x(value, turn):
    def partner(x, core):
        return (x + 1 if (x + core + turn) % 2 == 0 else x - 1) % 4

    pairs = [(x * 2 + core, partner(x, core) * 2 + core) for x in range(4) for core in range(2)]
    return lax.ppermute(value, ("xh", "xl", "c"), pairs)


def prepare(inputs, out_grads):
    both = jnp.stack([inputs, out_grads])
    padded = jnp.pad(both, ((0, 0), (0, 0), (0, 0), (0, 2), (0, 0)))
    return padded.reshape(2, inputs.shape[0], 224, 256)


def take_patches(group, rows, patches, blocks):
    for n in range(4):
        feature = group[0, n].astype(F32)
        rows[n, 0, 16:240, :] = pltpu.roll(feature, 1, 0).astype(BF16)
        rows[n, 1, 16:240, :] = group[0, n]
        rows[n, 2, 16:240, :] = pltpu.roll(feature, 223, 0).astype(BF16)
        at = slice(256 * n, 256 * n + 256)
        for tap in range(9):
            ky, kx = tap // 3, tap % 3
            shifted = rows[n, kx, 16 * ky : 16 * ky + 256, :]
            if tap <= 4 and 0 in blocks:
                last = min(256 * tap + 256, 1152)
                patches[0, at, 256 * tap : last] = shifted[:, : last - 256 * tap]
            if tap >= 4 and 1 in blocks:
                first = max(256 * tap - 1152, 0)
                patches[1, at, first : 256 * tap - 896] = shifted[:, first + 1152 - 256 * tap :]


def clear_edges(rows):
    rows[:, :, 0:16, :] = jnp.zeros((4, 3, 16, 256), BF16)
    rows[:, :, 240:288, :] = jnp.zeros((4, 3, 48, 256), BF16)


def rotate(basis, patches):
    return lax.dot_general(
        basis, patches, CONTRACT_LAST, preferred_element_type=F32
    ).astype(BF16)


def rotate_grads(group, out_basis, grads):
    for n in range(4):
        grads[n, 0:224, :] = lax.dot_general(
            group[1, n], out_basis[...], CONTRACT_LAST, preferred_element_type=F32
        ).astype(BF16)


def add_moments(rotated, grads, squares_ref, linear_ref, block):
    squares, linear = squares_ref[block], linear_ref[block]
    for n in range(4):
        projected = jnp.dot(
            rotated[:, 256 * n : 256 * n + 256], grads[n], preferred_element_type=F32
        )
        squares = squares + projected * projected
        linear = linear + projected
    squares_ref[block] = squares
    linear_ref[block] = linear


def first_kernel(own, other, here, plus, minus, rotated, basis, rows, patches):
    y = lax.axis_index("y")
    odd = lax.rem(y, 2)
    basis[pl.ds(pl.multiple_of(odd * 144, 16), 144), :] = here[...]
    basis[pl.ds(pl.multiple_of(144 - odd * 144, 16), 144), :] = jnp.where(
        odd == 0, plus[...], minus[...]
    )
    clear_edges(rows)
    for block in range(2):

        @pl.when(y // 2 == block)
        def _(block=block):
            for at, group in enumerate((own, other)):
                take_patches(group, rows, patches, (block,))
                rotated[at] = rotate(basis[...], patches[block])


def near_kernel(
    own, other, rotated, first, plus, minus, two_top, two_bottom, u_here, u_two,
    squares_ref, linear_ref, basis, out_basis, rows, patches, grads,
):
    y, xl, core = lax.axis_index("y"), lax.axis_index("xl"), lax.axis_index("c")
    odd, own_block = lax.rem(y, 2), y // 2
    at = odd * 144
    basis[own_block] = first[...]
    second = basis.at[1 - own_block]
    second[pl.ds(pl.multiple_of(at, 16), TOP), :] = two_top[0:TOP, :]
    second[pl.ds(pl.multiple_of(at + TOP, 16), 144 - TOP), :] = two_bottom[0 : 144 - TOP, :]
    second[pl.ds(pl.multiple_of(144 - at, 16), 144), :] = jnp.where(
        odd == 0, minus[...], plus[...]
    )
    for dy, (source, row) in enumerate(
        ((u_here, 0), (two_top, TOP), (u_two, 0), (two_bottom, 144 - TOP))
    ):
        for piece in range(4):
            dc, dx = piece // 2, piece % 2
            owner = (lax.rem(y + dy, 4) * 2 + lax.rem(xl + dx, 2)) * 2 + lax.rem(core + dc, 2)
            place = owner % 2 * 128 + owner // 2 * 16
            out_basis[pl.ds(pl.multiple_of(place, 16), 16), :] = source[
                row : row + 16, 256 * piece : 256 * piece + 256
            ]
    clear_edges(rows)
    grads[:, 224:256, :] = jnp.zeros((4, 32, 256), BF16)
    squares_ref[...] = jnp.zeros_like(squares_ref)
    linear_ref[...] = jnp.zeros_like(linear_ref)
    for block in range(2):

        @pl.when(own_block == block)
        def _(block=block):
            for n, group in enumerate((own, other)):
                take_patches(group, rows, patches, (1 - block,))
                rotate_grads(group, out_basis, grads)
                add_moments(rotated[n], grads, squares_ref, linear_ref, block)
                add_moments(
                    rotate(basis[1 - block], patches[1 - block]),
                    grads, squares_ref, linear_ref, 1 - block,
                )


def far_kernel(
    far, far_other, squares_in, linear_in, basis, out_basis,
    sums, squares_ref, linear_ref, rows, patches, grads,
):
    clear_edges(rows)
    grads[:, 224:256, :] = jnp.zeros((4, 32, 256), BF16)
    squares_ref[...] = squares_in[...]
    linear_ref[...] = linear_in[...]
    for group in (far, far_other):
        take_patches(group, rows, patches, (0, 1))
        rotate_grads(group, out_basis, grads)
        for block in range(2):
            add_moments(
                rotate(basis[block], patches[block]), grads, squares_ref, linear_ref, block
            )
    for owner in range(4):
        at = slice(144 * (owner % 2), 144 * (owner % 2) + 144)
        for half in range(2):
            lanes = slice(128 * half, 128 * half + 128)
            sums[4 * half + owner, 0] = squares_ref[owner // 2, at, lanes].astype(BF16)
            sums[4 * half + owner, 1] = linear_ref[owner // 2, at, lanes].astype(BF16)


def call(kernel, name, flops, out_shape, scratch, *operands):
    vmem = pl.BlockSpec(memory_space=pltpu.VMEM)
    return pl.pallas_call(
        kernel,
        out_shape=out_shape,
        in_specs=[vmem] * len(operands),
        out_specs=jax.tree.map(lambda _: vmem, out_shape),
        scratch_shapes=scratch,
        compiler_params=pltpu.CompilerParams(vmem_limit_bytes=20 * 2**20),
        cost_estimate=pl.CostEstimate(flops=flops, bytes_accessed=10**6, transcendentals=0),
        name=name,
    )(*operands)


def forward_kernel(plus, minus, eigenvectors, top, bottom):
    top[0:TOP, :] = plus[0:TOP, :]
    bottom[0 : 144 - TOP, :] = minus[TOP:144, :]
    for target, row in ((top, TOP), (bottom, 144 - TOP)):
        target[row : row + 16, 0:1024] = eigenvectors[...]
        target[row : row + 16, 1024:1152] = jnp.zeros((16, 128), BF16)


def on_device(inputs, out_grads, patch_basis, output_basis):
    examples = inputs.shape[0] * math.prod(SIZES)
    side = inputs.shape[1]

    shard = patch_basis.T
    plus, minus = ring(shard, "y", 4, 3), ring(shard, "y", 4, 1)
    u0 = output_basis.T
    own = prepare(inputs, out_grads)
    u_x = swap_x(u0, 0)
    _, u_x = lax.optimization_barrier((own, u_x))
    u1 = jnp.concatenate([u0, u_x], axis=1)
    u2 = jnp.concatenate([u1, swap_cores(u1)], axis=1)
    top, bottom = call(
        forward_kernel,
        "forward",
        13*10**9,
        tuple(jax.ShapeDtypeStruct((n + 16, 1152), BF16) for n in (TOP, 144 - TOP)),
        [],
        plus, minus, u2,
    )
    two_top, two_bottom = ring(top, "y", 4, 3), ring(bottom, "y", 4, 1)
    u_two = ring(u2, "y", 4, 2)
    other = swap_cores(own)
    far = swap_x(own, 0)

    moment = jax.ShapeDtypeStruct((2, 288, 256), F32)
    rows, patches = pltpu.VMEM((4, 3, 288, 256), BF16), pltpu.VMEM((2, 1024, 1152), BF16)
    grads = pltpu.VMEM((4, 256, 256), BF16)
    rotated, first = call(
        first_kernel,
        "first_block_near",
        4*10**9,
        (
            jax.ShapeDtypeStruct((2, 288, 1024), BF16),
            jax.ShapeDtypeStruct((288, 1152), BF16),
        ),
        [rows, patches],
        own, other, shard, plus, minus,
    )
    far, two_top, two_bottom, u_two, rotated = lax.optimization_barrier(
        (far, two_top, two_bottom, u_two, rotated)
    )
    far_other = swap_cores(far)
    squares, linear, basis, out_basis = call(
        near_kernel,
        "near_examples",
        4 * 10**9,
        (
            moment,
            moment,
            jax.ShapeDtypeStruct((2, 288, 1152), BF16),
            jax.ShapeDtypeStruct((256, 256), BF16),
        ),
        [rows, patches, grads],
        own, other, rotated, first, plus, minus, two_top, two_bottom, u2, u_two,
    )
    sums = call(
        far_kernel,
        "far_examples",
        4 * 10**9,
        jax.ShapeDtypeStruct((8, 2, 144, 128), BF16),
        [pltpu.VMEM((2, 288, 256), F32)] * 2 + [rows, patches, grads],
        far, far_other, squares, linear, basis, out_basis,
    )

    sums = lax.all_to_all(sums, ("xh", "y"), 0, 0, tiled=True)
    sums = jnp.sum(sums.astype(F32), axis=0).reshape(288, 128).T.astype(BF16)
    sums = lax.all_to_all(sums, ("zh", "zl"), 0, 0, tiled=True)
    sums = jnp.sum(sums.reshape(8, 16, 288).astype(F32), axis=0)
    return (
        sums[:, :144] * (1.0 / (side * side * examples)),
        sums[:, 144:] * (1.0 / (side * math.sqrt(examples))),
    )


def solution(mesh):
    fine = Mesh(mesh.devices.reshape(SIZES), AXES)
    every, columns, rows = AXES, AXES[3:], AXES[:3]
    return jax.shard_map(
        on_device,
        mesh=fine,
        in_specs=(P(every), P(every), P(None, columns), P(None, columns)),
        out_specs=(P(rows, columns), P(rows, columns)),
        check_vma=False,
    )
```

```python
import math

import jax
import jax.numpy as jnp
from jax import lax
from jax.experimental import pallas as pl
from jax.experimental.pallas import tpu as pltpu
from jax.sharding import Mesh, PartitionSpec as P

AXES = ("zh", "zl", "xh", "y", "xl", "c")
SIZES = (4, 2, 2, 4, 2, 2)
BF16 = jnp.bfloat16
F32 = jnp.float32
CONTRACT_LAST = (((1,), (1,)), ((), ()))
TOP = 80


def ring(value, axis, size, step):
    return lax.ppermute(value, axis, [(i, (i + step) % size) for i in range(size)])


def swap_cores(value):
    return lax.ppermute(value, "c", [(0, 1), (1, 0)])


def swap_x(value, turn):
    def partner(x, core):
        return (x + 1 if (x + core + turn) % 2 == 0 else x - 1) % 4

    pairs = [(x * 2 + core, partner(x, core) * 2 + core) for x in range(4) for core in range(2)]
    return lax.ppermute(value, ("xh", "xl", "c"), pairs)


def prepare(inputs, out_grads):
    both = jnp.stack([inputs, out_grads])
    padded = jnp.pad(both, ((0, 0), (0, 0), (0, 0), (0, 2), (0, 0)))
    return padded.reshape(2, inputs.shape[0], 224, 256)


def take_patches(group, rows, patches, blocks):
    for n in range(4):
        feature = group[0, n].astype(F32)
        rows[n, 0, 16:240, :] = pltpu.roll(feature, 1, 0).astype(BF16)
        rows[n, 1, 16:240, :] = group[0, n]
        rows[n, 2, 16:240, :] = pltpu.roll(feature, 223, 0).astype(BF16)
        at = slice(256 * n, 256 * n + 256)
        for tap in range(9):
            ky, kx = tap // 3, tap % 3
            shifted = rows[n, kx, 16 * ky : 16 * ky + 256, :]
            if tap <= 4 and 0 in blocks:
                last = min(256 * tap + 256, 1152)
                patches[0, at, 256 * tap : last] = shifted[:, : last - 256 * tap]
            if tap >= 4 and 1 in blocks:
                first = max(256 * tap - 1152, 0)
                patches[1, at, first : 256 * tap - 896] = shifted[:, first + 1152 - 256 * tap :]


def clear_edges(rows):
    rows[:, :, 0:16, :] = jnp.zeros((4, 3, 16, 256), BF16)
    rows[:, :, 240:288, :] = jnp.zeros((4, 3, 48, 256), BF16)


def rotate(basis, patches):
    return lax.dot_general(
        basis, patches, CONTRACT_LAST, preferred_element_type=F32
    ).astype(BF16)


def rotate_grads(group, out_basis, grads):
    for n in range(4):
        grads[n, 0:224, :] = lax.dot_general(
            group[1, n], out_basis[...], CONTRACT_LAST, preferred_element_type=F32
        ).astype(BF16)


def add_moments(rotated, grads, squares_ref, linear_ref, block):
    squares, linear = squares_ref[block], linear_ref[block]
    for n in range(4):
        projected = jnp.dot(
            rotated[:, 256 * n : 256 * n + 256], grads[n], preferred_element_type=F32
        )
        squares = squares + projected * projected
        linear = linear + projected
    squares_ref[block] = squares
    linear_ref[block] = linear


def first_kernel(own, other, here, plus, minus, rotated, basis, rows, patches):
    y = lax.axis_index("y")
    odd = lax.rem(y, 2)
    basis[pl.ds(pl.multiple_of(odd * 144, 16), 144), :] = here[...]
    basis[pl.ds(pl.multiple_of(144 - odd * 144, 16), 144), :] = jnp.where(
        odd == 0, plus[...], minus[...]
    )
    clear_edges(rows)
    for block in range(2):

        @pl.when(y // 2 == block)
        def _(block=block):
            for at, group in enumerate((own, other)):
                take_patches(group, rows, patches, (block,))
                rotated[at] = rotate(basis[...], patches[block])


def near_kernel(
    own, other, rotated, first, plus, minus, two_top, two_bottom, u_here, u_two,
    squares_ref, linear_ref, basis, out_basis, rows, patches, grads,
):
    y, xl, core = lax.axis_index("y"), lax.axis_index("xl"), lax.axis_index("c")
    odd, own_block = lax.rem(y, 2), y // 2
    at = odd * 144
    basis[own_block] = first[...]
    second = basis.at[1 - own_block]
    second[pl.ds(pl.multiple_of(at, 16), TOP), :] = two_top[0:TOP, :]
    second[pl.ds(pl.multiple_of(at + TOP, 16), 144 - TOP), :] = two_bottom[0 : 144 - TOP, :]
    second[pl.ds(pl.multiple_of(144 - at, 16), 144), :] = jnp.where(
        odd == 0, minus[...], plus[...]
    )
    for dy, (source, row) in enumerate(
        ((u_here, 0), (two_top, TOP), (u_two, 0), (two_bottom, 144 - TOP))
    ):
        for piece in range(4):
            dc, dx = piece // 2, piece % 2
            owner = (lax.rem(y + dy, 4) * 2 + lax.rem(xl + dx, 2)) * 2 + lax.rem(core + dc, 2)
            place = owner % 2 * 128 + owner // 2 * 16
            out_basis[pl.ds(pl.multiple_of(place, 16), 16), :] = source[
                row : row + 16, 256 * piece : 256 * piece + 256
            ]
    clear_edges(rows)
    grads[:, 224:256, :] = jnp.zeros((4, 32, 256), BF16)
    squares_ref[...] = jnp.zeros_like(squares_ref)
    linear_ref[...] = jnp.zeros_like(linear_ref)
    for block in range(2):

        @pl.when(own_block == block)
        def _(block=block):
            for n, group in enumerate((own, other)):
                take_patches(group, rows, patches, (1 - block,))
                rotate_grads(group, out_basis, grads)
                add_moments(rotated[n], grads, squares_ref, linear_ref, block)
                add_moments(
                    rotate(basis[1 - block], patches[1 - block]),
                    grads, squares_ref, linear_ref, 1 - block,
                )


def far_kernel(
    far, far_other, squares_in, linear_in, basis, out_basis,
    sums, squares_ref, linear_ref, rows, patches, grads,
):
    clear_edges(rows)
    grads[:, 224:256, :] = jnp.zeros((4, 32, 256), BF16)
    squares_ref[...] = squares_in[...]
    linear_ref[...] = linear_in[...]
    for group in (far, far_other):
        take_patches(group, rows, patches, (0, 1))
        rotate_grads(group, out_basis, grads)
        for block in range(2):
            add_moments(
                rotate(basis[block], patches[block]), grads, squares_ref, linear_ref, block
            )
    for owner in range(4):
        at = slice(144 * (owner % 2), 144 * (owner % 2) + 144)
        for half in range(2):
            lanes = slice(128 * half, 128 * half + 128)
            sums[2 * owner + half, 0] = squares_ref[owner // 2, at, lanes].astype(BF16)
            sums[2 * owner + half, 1] = linear_ref[owner // 2, at, lanes].astype(BF16)


def call(kernel, name, flops, out_shape, scratch, *operands):
    vmem = pl.BlockSpec(memory_space=pltpu.VMEM)
    return pl.pallas_call(
        kernel,
        out_shape=out_shape,
        in_specs=[vmem] * len(operands),
        out_specs=jax.tree.map(lambda _: vmem, out_shape),
        scratch_shapes=scratch,
        compiler_params=pltpu.CompilerParams(vmem_limit_bytes=20 * 2**20),
        cost_estimate=pl.CostEstimate(flops=flops, bytes_accessed=10**6, transcendentals=0),
        name=name,
    )(*operands)


def forward_kernel(plus, minus, eigenvectors, top, bottom):
    top[0:TOP, :] = plus[0:TOP, :]
    bottom[0 : 144 - TOP, :] = minus[TOP:144, :]
    for target, row in ((top, TOP), (bottom, 144 - TOP)):
        target[row : row + 16, 0:1024] = eigenvectors[...]
        target[row : row + 16, 1024:1152] = jnp.zeros((16, 128), BF16)


def on_device(inputs, out_grads, patch_basis, output_basis):
    examples = inputs.shape[0] * math.prod(SIZES)
    side = inputs.shape[1]

    shard = patch_basis.T
    plus, minus = ring(shard, "y", 4, 3), ring(shard, "y", 4, 1)
    u0 = output_basis.T
    own = prepare(inputs, out_grads)
    u_x = swap_x(u0, 0)
    _, u_x = lax.optimization_barrier((own, u_x))
    u1 = jnp.concatenate([u0, u_x], axis=1)
    u2 = jnp.concatenate([u1, swap_cores(u1)], axis=1)
    top, bottom = call(
        forward_kernel,
        "forward",
        13*10**9,
        tuple(jax.ShapeDtypeStruct((n + 16, 1152), BF16) for n in (TOP, 144 - TOP)),
        [],
        plus, minus, u2,
    )
    two_top, two_bottom = ring(top, "y", 4, 3), ring(bottom, "y", 4, 1)
    u_two = ring(u2, "y", 4, 2)
    late, _ = lax.optimization_barrier((own, u2))
    other = swap_cores(late)
    far = swap_x(own, 0)

    moment = jax.ShapeDtypeStruct((2, 288, 256), F32)
    rows, patches = pltpu.VMEM((4, 3, 288, 256), BF16), pltpu.VMEM((2, 1024, 1152), BF16)
    grads = pltpu.VMEM((4, 256, 256), BF16)
    rotated, first = call(
        first_kernel,
        "first_block_near",
        4*10**9,
        (
            jax.ShapeDtypeStruct((2, 288, 1024), BF16),
            jax.ShapeDtypeStruct((288, 1152), BF16),
        ),
        [rows, patches],
        own, other, shard, plus, minus,
    )
    far, two_top, two_bottom, u_two, rotated = lax.optimization_barrier(
        (far, two_top, two_bottom, u_two, rotated)
    )
    far_other = swap_cores(far)
    squares, linear, basis, out_basis = call(
        near_kernel,
        "near_examples",
        4 * 10**9,
        (
            moment,
            moment,
            jax.ShapeDtypeStruct((2, 288, 1152), BF16),
            jax.ShapeDtypeStruct((256, 256), BF16),
        ),
        [rows, patches, grads],
        own, other, rotated, first, plus, minus, two_top, two_bottom, u2, u_two,
    )
    sums = call(
        far_kernel,
        "far_examples",
        4 * 10**9,
        jax.ShapeDtypeStruct((8, 2, 144, 128), BF16),
        [pltpu.VMEM((2, 288, 256), F32)] * 2 + [rows, patches, grads],
        far, far_other, squares, linear, basis, out_basis,
    )

    sums = lax.all_to_all(sums, ("y", "xh"), 0, 0, tiled=True)
    sums = jnp.sum(sums.astype(F32), axis=0).reshape(288, 128).T.astype(BF16)
    sums = lax.all_to_all(sums, ("zh", "zl"), 0, 0, tiled=True)
    sums = jnp.sum(sums.reshape(8, 16, 288).astype(F32), axis=0)
    return (
        sums[:, :144] * (1.0 / (side * side * examples)),
        sums[:, 144:] * (1.0 / (side * math.sqrt(examples))),
    )


def solution(mesh):
    fine = Mesh(mesh.devices.reshape(SIZES), AXES)
    every, columns, rows = AXES, AXES[3:], AXES[:3]
    return jax.shard_map(
        on_device,
        mesh=fine,
        in_specs=(P(every), P(every), P(None, columns), P(None, columns)),
        out_specs=(P(rows, columns), P(rows, columns)),
        check_vma=False,
    )
```

```python
import math

import jax
import jax.numpy as jnp
from jax import lax
from jax.experimental import pallas as pl
from jax.experimental.pallas import tpu as pltpu
from jax.sharding import Mesh, PartitionSpec as P

AXES = ("zh", "zl", "xh", "y", "xl", "c")
SIZES = (4, 2, 2, 4, 2, 2)
BF16 = jnp.bfloat16
F32 = jnp.float32
CONTRACT_LAST = (((1,), (1,)), ((), ()))
TOP = 80


def ring(value, axis, size, step):
    return lax.ppermute(value, axis, [(i, (i + step) % size) for i in range(size)])


def swap_cores(value):
    return lax.ppermute(value, "c", [(0, 1), (1, 0)])


def swap_x(value, turn):
    def partner(x, core):
        return (x + 1 if (x + core + turn) % 2 == 0 else x - 1) % 4

    pairs = [(x * 2 + core, partner(x, core) * 2 + core) for x in range(4) for core in range(2)]
    return lax.ppermute(value, ("xh", "xl", "c"), pairs)


def prepare(inputs, out_grads):
    both = jnp.stack([inputs, out_grads])
    padded = jnp.pad(both, ((0, 0), (0, 0), (0, 0), (0, 2), (0, 0)))
    return padded.reshape(2, inputs.shape[0], 224, 256)


def take_patches(group, rows, patches, blocks):
    for n in range(4):
        feature = group[0, n].astype(F32)
        rows[n, 0, 16:240, :] = pltpu.roll(feature, 1, 0).astype(BF16)
        rows[n, 1, 16:240, :] = group[0, n]
        rows[n, 2, 16:240, :] = pltpu.roll(feature, 223, 0).astype(BF16)
        at = slice(256 * n, 256 * n + 256)
        for tap in range(9):
            ky, kx = tap // 3, tap % 3
            shifted = rows[n, kx, 16 * ky : 16 * ky + 256, :]
            if tap <= 4 and 0 in blocks:
                last = min(256 * tap + 256, 1152)
                patches[0, at, 256 * tap : last] = shifted[:, : last - 256 * tap]
            if tap >= 4 and 1 in blocks:
                first = max(256 * tap - 1152, 0)
                patches[1, at, first : 256 * tap - 896] = shifted[:, first + 1152 - 256 * tap :]


def clear_edges(rows):
    rows[:, :, 0:16, :] = jnp.zeros((4, 3, 16, 256), BF16)
    rows[:, :, 240:288, :] = jnp.zeros((4, 3, 48, 256), BF16)


def rotate(basis, patches):
    return lax.dot_general(
        basis, patches, CONTRACT_LAST, preferred_element_type=F32
    ).astype(BF16)


def rotate_grads(group, out_basis, grads):
    for n in range(4):
        grads[n, 0:224, :] = lax.dot_general(
            group[1, n], out_basis[...], CONTRACT_LAST, preferred_element_type=F32
        ).astype(BF16)


def add_moments(rotated, grads, squares_ref, linear_ref, block):
    squares, linear = squares_ref[block], linear_ref[block]
    for n in range(4):
        projected = jnp.dot(
            rotated[:, 256 * n : 256 * n + 256], grads[n], preferred_element_type=F32
        )
        squares = squares + projected * projected
        linear = linear + projected
    squares_ref[block] = squares
    linear_ref[block] = linear


def first_kernel(own, other, here, plus, minus, rotated, basis, rows, patches):
    y = lax.axis_index("y")
    odd = lax.rem(y, 2)
    basis[pl.ds(pl.multiple_of(odd * 144, 16), 144), :] = here[...]
    basis[pl.ds(pl.multiple_of(144 - odd * 144, 16), 144), :] = jnp.where(
        odd == 0, plus[...], minus[...]
    )
    clear_edges(rows)
    for block in range(2):

        @pl.when(y // 2 == block)
        def _(block=block):
            for at, group in enumerate((own, other)):
                take_patches(group, rows, patches, (block,))
                rotated[at] = rotate(basis[...], patches[block])


def near_kernel(
    own, other, rotated, first, plus, minus, two_top, two_bottom, u_here, u_two,
    squares_ref, linear_ref, basis, out_basis, rows, patches, grads,
):
    y, xl, core = lax.axis_index("y"), lax.axis_index("xl"), lax.axis_index("c")
    odd, own_block = lax.rem(y, 2), y // 2
    at = odd * 144
    basis[own_block] = first[...]
    second = basis.at[1 - own_block]
    second[pl.ds(pl.multiple_of(at, 16), TOP), :] = two_top[0:TOP, :]
    second[pl.ds(pl.multiple_of(at + TOP, 16), 144 - TOP), :] = two_bottom[0 : 144 - TOP, :]
    second[pl.ds(pl.multiple_of(144 - at, 16), 144), :] = jnp.where(
        odd == 0, minus[...], plus[...]
    )
    for dy, (source, row) in enumerate(
        ((u_here, 0), (two_top, TOP), (u_two, 0), (two_bottom, 144 - TOP))
    ):
        for piece in range(4):
            dc, dx = piece // 2, piece % 2
            owner = (lax.rem(y + dy, 4) * 2 + lax.rem(xl + dx, 2)) * 2 + lax.rem(core + dc, 2)
            place = owner % 2 * 128 + owner // 2 * 16
            out_basis[pl.ds(pl.multiple_of(place, 16), 16), :] = source[
                row : row + 16, 256 * piece : 256 * piece + 256
            ]
    clear_edges(rows)
    grads[:, 224:256, :] = jnp.zeros((4, 32, 256), BF16)
    squares_ref[...] = jnp.zeros_like(squares_ref)
    linear_ref[...] = jnp.zeros_like(linear_ref)
    for block in range(2):

        @pl.when(own_block == block)
        def _(block=block):
            for n, group in enumerate((own, other)):
                take_patches(group, rows, patches, (1 - block,))
                rotate_grads(group, out_basis, grads)
                add_moments(rotated[n], grads, squares_ref, linear_ref, block)
                add_moments(
                    rotate(basis[1 - block], patches[1 - block]),
                    grads, squares_ref, linear_ref, 1 - block,
                )


def far_kernel(
    far, squares_in, linear_in, basis, out_basis, squares_ref, linear_ref, rows, patches, grads
):
    clear_edges(rows)
    grads[:, 224:256, :] = jnp.zeros((4, 32, 256), BF16)
    squares_ref[...] = squares_in[...]
    linear_ref[...] = linear_in[...]
    take_patches(far, rows, patches, (0, 1))
    rotate_grads(far, out_basis, grads)
    for block in range(2):
        add_moments(rotate(basis[block], patches[block]), grads, squares_ref, linear_ref, block)


def last_kernel(
    far, squares_in, linear_in, basis, out_basis, sums, squares_ref, linear_ref, *scratch
):
    far_kernel(
        far, squares_in, linear_in, basis, out_basis, squares_ref, linear_ref, *scratch
    )
    for owner in range(4):
        at = slice(144 * (owner % 2), 144 * (owner % 2) + 144)
        for half in range(2):
            lanes = slice(128 * half, 128 * half + 128)
            sums[2 * owner + half, 0] = squares_ref[owner // 2, at, lanes].astype(BF16)
            sums[2 * owner + half, 1] = linear_ref[owner // 2, at, lanes].astype(BF16)


def call(kernel, name, flops, out_shape, scratch, *operands):
    vmem = pl.BlockSpec(memory_space=pltpu.VMEM)
    return pl.pallas_call(
        kernel,
        out_shape=out_shape,
        in_specs=[vmem] * len(operands),
        out_specs=jax.tree.map(lambda _: vmem, out_shape),
        scratch_shapes=scratch,
        compiler_params=pltpu.CompilerParams(vmem_limit_bytes=20 * 2**20),
        cost_estimate=pl.CostEstimate(flops=flops, bytes_accessed=10**6, transcendentals=0),
        name=name,
    )(*operands)


def forward_kernel(plus, minus, eigenvectors, top, bottom):
    top[0:TOP, :] = plus[0:TOP, :]
    bottom[0 : 144 - TOP, :] = minus[TOP:144, :]
    for target, row in ((top, TOP), (bottom, 144 - TOP)):
        target[row : row + 16, 0:1024] = eigenvectors[...]
        target[row : row + 16, 1024:1152] = jnp.zeros((16, 128), BF16)


def on_device(inputs, out_grads, patch_basis, output_basis):
    examples = inputs.shape[0] * math.prod(SIZES)
    side = inputs.shape[1]

    shard = patch_basis.T
    plus, minus = ring(shard, "y", 4, 3), ring(shard, "y", 4, 1)
    u0 = output_basis.T
    own = prepare(inputs, out_grads)
    u_x = swap_x(u0, 0)
    _, u_x = lax.optimization_barrier((own, u_x))
    u1 = jnp.concatenate([u0, u_x], axis=1)
    u2 = jnp.concatenate([u1, swap_cores(u1)], axis=1)
    top, bottom = call(
        forward_kernel,
        "forward",
        13*10**9,
        tuple(jax.ShapeDtypeStruct((n + 16, 1152), BF16) for n in (TOP, 144 - TOP)),
        [],
        plus, minus, u2,
    )
    two_top, two_bottom = ring(top, "y", 4, 3), ring(bottom, "y", 4, 1)
    u_two = ring(u2, "y", 4, 2)
    late, _ = lax.optimization_barrier((own, u2))
    other = swap_cores(late)
    far = swap_x(own, 0)

    moment = jax.ShapeDtypeStruct((2, 288, 256), F32)
    rows, patches = pltpu.VMEM((4, 3, 288, 256), BF16), pltpu.VMEM((2, 1024, 1152), BF16)
    grads = pltpu.VMEM((4, 256, 256), BF16)
    rotated, first = call(
        first_kernel,
        "first_block_near",
        4*10**9,
        (
            jax.ShapeDtypeStruct((2, 288, 1024), BF16),
            jax.ShapeDtypeStruct((288, 1152), BF16),
        ),
        [rows, patches],
        own, other, shard, plus, minus,
    )
    squares, linear, basis, out_basis = call(
        near_kernel,
        "near_examples",
        4 * 10**9,
        (
            moment,
            moment,
            jax.ShapeDtypeStruct((2, 288, 1152), BF16),
            jax.ShapeDtypeStruct((256, 256), BF16),
        ),
        [rows, patches, grads],
        own, other, rotated, first, plus, minus, two_top, two_bottom, u2, u_two,
    )
    far, squares = lax.optimization_barrier((far, squares))
    far_other = swap_cores(far)
    squares, linear = call(
        far_kernel,
        "far_examples",
        4 * 10**9,
        (moment, moment),
        [rows, patches, grads],
        far, squares, linear, basis, out_basis,
    )
    sums = call(
        last_kernel,
        "last_examples",
        2 * 10**9,
        jax.ShapeDtypeStruct((8, 2, 144, 128), BF16),
        [pltpu.VMEM((2, 288, 256), F32)] * 2 + [rows, patches, grads],
        far_other, squares, linear, basis, out_basis,
    )

    sums = lax.all_to_all(sums, ("y", "xh"), 0, 0, tiled=True)
    sums = jnp.sum(sums.astype(F32), axis=0).reshape(288, 128).T.astype(BF16)
    sums = lax.all_to_all(sums, ("zh", "zl"), 0, 0, tiled=True)
    sums = jnp.sum(sums.reshape(8, 16, 288).astype(F32), axis=0)
    return (
        sums[:, :144] * (1.0 / (side * side * examples)),
        sums[:, 144:] * (1.0 / (side * math.sqrt(examples))),
    )


def solution(mesh):
    fine = Mesh(mesh.devices.reshape(SIZES), AXES)
    every, columns, rows = AXES, AXES[3:], AXES[:3]
    return jax.shard_map(
        on_device,
        mesh=fine,
        in_specs=(P(every), P(every), P(None, columns), P(None, columns)),
        out_specs=(P(rows, columns), P(rows, columns)),
        check_vma=False,
    )
```

```python
import math

import jax
import jax.numpy as jnp
from jax import lax
from jax.experimental import pallas as pl
from jax.experimental.pallas import tpu as pltpu
from jax.sharding import Mesh, PartitionSpec as P

AXES = ("zh", "zl", "xh", "y", "xl", "c")
SIZES = (4, 2, 2, 4, 2, 2)
BF16 = jnp.bfloat16
F32 = jnp.float32
CONTRACT_LAST = (((1,), (1,)), ((), ()))
TOP = 80


def ring(value, axis, size, step):
    return lax.ppermute(value, axis, [(i, (i + step) % size) for i in range(size)])


def swap_cores(value):
    return lax.ppermute(value, "c", [(0, 1), (1, 0)])


def swap_x(value, turn):
    def partner(x, core):
        return (x + 1 if (x + core + turn) % 2 == 0 else x - 1) % 4

    pairs = [(x * 2 + core, partner(x, core) * 2 + core) for x in range(4) for core in range(2)]
    return lax.ppermute(value, ("xh", "xl", "c"), pairs)


def prepare(inputs, out_grads):
    both = jnp.stack([inputs, out_grads])
    padded = jnp.pad(both, ((0, 0), (0, 0), (0, 0), (0, 2), (0, 0)))
    return padded.reshape(2, inputs.shape[0], 224, 256)


def take_patches(group, rows, patches, blocks):
    for n in range(4):
        feature = group[0, n].astype(F32)
        rows[n, 0, 16:240, :] = pltpu.roll(feature, 1, 0).astype(BF16)
        rows[n, 1, 16:240, :] = group[0, n]
        rows[n, 2, 16:240, :] = pltpu.roll(feature, 223, 0).astype(BF16)
        at = slice(256 * n, 256 * n + 256)
        for tap in range(9):
            ky, kx = tap // 3, tap % 3
            shifted = rows[n, kx, 16 * ky : 16 * ky + 256, :]
            if tap <= 4 and 0 in blocks:
                last = min(256 * tap + 256, 1152)
                patches[0, at, 256 * tap : last] = shifted[:, : last - 256 * tap]
            if tap >= 4 and 1 in blocks:
                first = max(256 * tap - 1152, 0)
                patches[1, at, first : 256 * tap - 896] = shifted[:, first + 1152 - 256 * tap :]


def clear_edges(rows):
    rows[:, :, 0:16, :] = jnp.zeros((4, 3, 16, 256), BF16)
    rows[:, :, 240:288, :] = jnp.zeros((4, 3, 48, 256), BF16)


def rotate(basis, patches):
    return lax.dot_general(
        basis, patches, CONTRACT_LAST, preferred_element_type=F32
    ).astype(BF16)


def rotate_grads(group, out_basis, grads):
    for n in range(4):
        grads[n, 0:224, :] = lax.dot_general(
            group[1, n], out_basis[...], CONTRACT_LAST, preferred_element_type=F32
        ).astype(BF16)


def add_moments(rotated, grads, squares_ref, linear_ref, block):
    squares, linear = squares_ref[block], linear_ref[block]
    for n in range(4):
        projected = jnp.dot(
            rotated[:, 256 * n : 256 * n + 256], grads[n], preferred_element_type=F32
        )
        squares = squares + projected * projected
        linear = linear + projected
    squares_ref[block] = squares
    linear_ref[block] = linear


def first_kernel(own, other, here, plus, minus, rotated, basis, rows, patches):
    y = lax.axis_index("y")
    odd = lax.rem(y, 2)
    basis[pl.ds(pl.multiple_of(odd * 144, 16), 144), :] = here[...]
    basis[pl.ds(pl.multiple_of(144 - odd * 144, 16), 144), :] = jnp.where(
        odd == 0, plus[...], minus[...]
    )
    clear_edges(rows)
    for block in range(2):

        @pl.when(y // 2 == block)
        def _(block=block):
            for at, group in enumerate((own, other)):
                take_patches(group, rows, patches, (block,))
                rotated[at] = rotate(basis[...], patches[block])


def near_kernel(
    own, other, rotated, first, plus, minus, two_top, two_bottom, u_here, u_two,
    squares_ref, linear_ref, basis, out_basis, rows, patches, grads,
):
    y, xl, core = lax.axis_index("y"), lax.axis_index("xl"), lax.axis_index("c")
    odd, own_block = lax.rem(y, 2), y // 2
    at = odd * 144
    basis[own_block] = first[...]
    second = basis.at[1 - own_block]
    second[pl.ds(pl.multiple_of(at, 16), TOP), :] = two_top[0:TOP, :]
    second[pl.ds(pl.multiple_of(at + TOP, 16), 144 - TOP), :] = two_bottom[0 : 144 - TOP, :]
    second[pl.ds(pl.multiple_of(144 - at, 16), 144), :] = jnp.where(
        odd == 0, minus[...], plus[...]
    )
    for dy, (source, row) in enumerate(
        ((u_here, 0), (two_top, TOP), (u_two, 0), (two_bottom, 144 - TOP))
    ):
        for piece in range(4):
            dc, dx = piece // 2, piece % 2
            owner = (lax.rem(y + dy, 4) * 2 + lax.rem(xl + dx, 2)) * 2 + lax.rem(core + dc, 2)
            place = owner % 2 * 128 + owner // 2 % 2 * 64 + owner // 4 * 16
            out_basis[pl.ds(pl.multiple_of(place, 16), 16), :] = source[
                row : row + 16, 256 * piece : 256 * piece + 256
            ]
    clear_edges(rows)
    grads[:, 224:256, :] = jnp.zeros((4, 32, 256), BF16)
    squares_ref[...] = jnp.zeros_like(squares_ref)
    linear_ref[...] = jnp.zeros_like(linear_ref)
    for block in range(2):

        @pl.when(own_block == block)
        def _(block=block):
            for n, group in enumerate((own, other)):
                take_patches(group, rows, patches, (1 - block,))
                rotate_grads(group, out_basis, grads)
                add_moments(rotated[n], grads, squares_ref, linear_ref, block)
                add_moments(
                    rotate(basis[1 - block], patches[1 - block]),
                    grads, squares_ref, linear_ref, 1 - block,
                )


def far_kernel(
    far, squares_in, linear_in, basis, out_basis, squares_ref, linear_ref, rows, patches, grads
):
    clear_edges(rows)
    grads[:, 224:256, :] = jnp.zeros((4, 32, 256), BF16)
    squares_ref[...] = squares_in[...]
    linear_ref[...] = linear_in[...]
    take_patches(far, rows, patches, (0, 1))
    rotate_grads(far, out_basis, grads)
    for block in range(2):
        add_moments(rotate(basis[block], patches[block]), grads, squares_ref, linear_ref, block)


def last_kernel(
    far, squares_in, linear_in, basis, out_basis, sums, squares_ref, linear_ref, *scratch
):
    far_kernel(
        far, squares_in, linear_in, basis, out_basis, squares_ref, linear_ref, *scratch
    )
    for owner in range(4):
        at = slice(144 * (owner % 2), 144 * (owner % 2) + 144)
        for half in range(2):
            lanes = slice(128 * half, 128 * half + 128)
            sums[2 * owner + half, 0] = squares_ref[owner // 2, at, lanes].astype(BF16)
            sums[2 * owner + half, 1] = linear_ref[owner // 2, at, lanes].astype(BF16)


def call(kernel, name, flops, out_shape, scratch, *operands):
    vmem = pl.BlockSpec(memory_space=pltpu.VMEM)
    return pl.pallas_call(
        kernel,
        out_shape=out_shape,
        in_specs=[vmem] * len(operands),
        out_specs=jax.tree.map(lambda _: vmem, out_shape),
        scratch_shapes=scratch,
        compiler_params=pltpu.CompilerParams(vmem_limit_bytes=20 * 2**20),
        cost_estimate=pl.CostEstimate(flops=flops, bytes_accessed=10**6, transcendentals=0),
        name=name,
    )(*operands)


def forward_kernel(plus, minus, eigenvectors, top, bottom):
    top[0:TOP, :] = plus[0:TOP, :]
    bottom[0 : 144 - TOP, :] = minus[TOP:144, :]
    for target, row in ((top, TOP), (bottom, 144 - TOP)):
        target[row : row + 16, 0:1024] = eigenvectors[...]
        target[row : row + 16, 1024:1152] = jnp.zeros((16, 128), BF16)


def on_device(inputs, out_grads, patch_basis, output_basis):
    examples = inputs.shape[0] * math.prod(SIZES)
    side = inputs.shape[1]

    shard = patch_basis.T
    plus, minus = ring(shard, "y", 4, 3), ring(shard, "y", 4, 1)
    u0 = output_basis.T
    own = prepare(inputs, out_grads)
    u_x = swap_x(u0, 0)
    _, u_x = lax.optimization_barrier((own, u_x))
    u1 = jnp.concatenate([u0, u_x], axis=1)
    u2 = jnp.concatenate([u1, swap_cores(u1)], axis=1)
    top, bottom = call(
        forward_kernel,
        "forward",
        13*10**9,
        tuple(jax.ShapeDtypeStruct((n + 16, 1152), BF16) for n in (TOP, 144 - TOP)),
        [],
        plus, minus, u2,
    )
    two_top, two_bottom = ring(top, "y", 4, 3), ring(bottom, "y", 4, 1)
    u_two = ring(u2, "y", 4, 2)
    late, _ = lax.optimization_barrier((own, u2))
    other = swap_cores(late)
    far = swap_x(own, 0)

    moment = jax.ShapeDtypeStruct((2, 288, 256), F32)
    rows, patches = pltpu.VMEM((4, 3, 288, 256), BF16), pltpu.VMEM((2, 1024, 1152), BF16)
    grads = pltpu.VMEM((4, 256, 256), BF16)
    rotated, first = call(
        first_kernel,
        "first_block_near",
        4*10**9,
        (
            jax.ShapeDtypeStruct((2, 288, 1024), BF16),
            jax.ShapeDtypeStruct((288, 1152), BF16),
        ),
        [rows, patches],
        own, other, shard, plus, minus,
    )
    squares, linear, basis, out_basis = call(
        near_kernel,
        "near_examples",
        4 * 10**9,
        (
            moment,
            moment,
            jax.ShapeDtypeStruct((2, 288, 1152), BF16),
            jax.ShapeDtypeStruct((256, 256), BF16),
        ),
        [rows, patches, grads],
        own, other, rotated, first, plus, minus, two_top, two_bottom, u2, u_two,
    )
    far, squares = lax.optimization_barrier((far, squares))
    far_other = swap_cores(far)
    squares, linear = call(
        far_kernel,
        "far_examples",
        4 * 10**9,
        (moment, moment),
        [rows, patches, grads],
        far, squares, linear, basis, out_basis,
    )
    sums = call(
        last_kernel,
        "last_examples",
        2 * 10**9,
        jax.ShapeDtypeStruct((8, 2, 144, 128), BF16),
        [pltpu.VMEM((2, 288, 256), F32)] * 2 + [rows, patches, grads],
        far_other, squares, linear, basis, out_basis,
    )

    sums = lax.all_to_all(sums, ("y", "xh"), 0, 0, tiled=True)
    sums = jnp.sum(sums.astype(F32), axis=0).reshape(288, 128).T.astype(BF16)
    sums = lax.all_to_all(sums, ("zl", "zh"), 0, 0, tiled=True)
    sums = jnp.sum(sums.reshape(8, 16, 288).astype(F32), axis=0)
    return (
        sums[:, :144] * (1.0 / (side * side * examples)),
        sums[:, 144:] * (1.0 / (side * math.sqrt(examples))),
    )


def solution(mesh):
    fine = Mesh(mesh.devices.reshape(SIZES), AXES)
    every, columns, rows = AXES, AXES[3:], AXES[:3]
    return jax.shard_map(
        on_device,
        mesh=fine,
        in_specs=(P(every), P(every), P(None, columns), P(None, columns)),
        out_specs=(P(rows, columns), P(rows, columns)),
        check_vma=False,
    )
```
